1024 devices in a mesh: tables: 64 (over z, core), cols: 16 (over y, x).
Axes of the slice: x: 4, y: 4, z: 32, core: 2. Of those that a mesh axis runs over, the one named last changes fastest.
Arguments:
- pooled_grad: bfloat16 [128, 1024, 8192], P(None, 'cols', 'tables'), may hold values from -6 to 6
- bag_ids: int32 [128, 8, 8192], P('tables'), may hold values from 0 to 1023
- bag_lengths: int32 [128, 8192], P('tables'), may hold values from 1 to 8
- table_rows: float32 [128, 1024, 1024], P('tables', 'cols'), may hold values from -6 to 6
- row_state: float32 [128, 1024], P('tables'), may hold values from 0.1 to 2
Outputs:
- new_rows: float32 [128, 1024, 1024], P('tables', 'cols')
- new_state: float32 [128, 1024], P('tables')
The draws below stay inside these ranges and needn't reach their ends.
Inputs may be any that keep to these rules, and one draw needn't show every extreme that they name: `bag_lengths`: ids at positions at or past a bag's length are ignored.
All inputs are finite; a program needn't handle non-finite values.
Results may differ from the reference program's by a relative error of at most 0.0003.
Values may be sent and summed in bfloat16 or wider, within the bound.
No kernel may reach another device: no remote copies, remote signals or barrier semaphores. Data moves between devices by JAX's collectives and lax.ppermute only.
A program may use at most 32 MiB of HBM per device.

```python
import math
import jax
import jax.numpy as jnp
from jax import lax

WIDTH = 1024
POOL = 8
ROWS = 1024
TABLES = 128
SAMPLES = 8192


def set_ends(drawn, rng, smallest, high):
    dims = drawn.shape
    spot = [jax.random.randint(jax.random.fold_in(rng, axis), (), 0, dims[axis]) for axis in range(len(dims))]
    drawn = drawn.at[tuple(spot)].set(smallest)
    longest = dims.index(max(dims))
    spot[longest] = (spot[longest] + 1) % dims[longest]
    return drawn.at[tuple(spot)].set(high)


def steps_of(rng, shape, split, least, high):
    loudness = 1.0
    for position, blocks in split:
        steps = jax.random.uniform(jax.random.fold_in(jax.random.fold_in(rng, 6), position), (blocks,), jnp.float32, least / len(split), high / len(split))
        loudness = loudness * jnp.repeat(jnp.exp(steps), shape[position] // blocks).reshape((-1,) + (1,) * (len(shape) - 1 - position))
    return loudness


def gaussian(rng, shape, spread, most, cuts=(), held_as=jnp.bfloat16):
    factor_of = steps_of(rng, shape, cuts, -0.22, 0.18) if cuts else 1.0
    array = jax.random.normal(rng, shape, jnp.float32) * spread * factor_of
    return jnp.minimum(jnp.maximum(array, -most), most).astype(held_as)


def setup_inputs(seed: int = 0) -> dict:
    key_list = jax.random.split(jax.random.key(seed), 6)
    return {
        "pooled_grad": gaussian(key_list[0], (TABLES, WIDTH, SAMPLES), 1.0, 6.0, ((1, 16), (2, 64))),
        "bag_ids": set_ends(jax.random.randint(key_list[1], (TABLES, POOL, SAMPLES), 0, ROWS), jax.random.fold_in(key_list[1], 1), 0, ROWS - 1).astype(jnp.int32),
        "bag_lengths": set_ends(jax.random.randint(key_list[2], (TABLES, SAMPLES), 1, POOL + 1), jax.random.fold_in(key_list[2], 1), 1, POOL).astype(jnp.int32),
        "table_rows": gaussian(key_list[3], (TABLES, WIDTH, ROWS), 1.0, 6.0, ((0, 64), (1, 16)), jnp.float32),
        "row_state": jnp.clip(jnp.exp(math.log(2.0) - 2.9957323 * jax.random.uniform(key_list[4], (TABLES, ROWS), jnp.float32) ** steps_of(key_list[4], (TABLES, ROWS), ((0, 64),), -0.2, 0.2)), 0.1, 2.0),
    }


learning_rate = 0.1
epsilon = 1e-06

def table_gradient(inputs):
    grads, row_ids, lengths_now = inputs
    columns_last = jnp.transpose(grads.astype(jnp.float32), (1, 0))
    total = jnp.zeros((ROWS, WIDTH), jnp.float32)
    for place in range(POOL):
        active = (place < lengths_now).astype(jnp.float32)
        weighted = columns_last * active[:, None]
        total = total + jax.ops.segment_sum(weighted, row_ids[place].astype(jnp.int32), num_segments=ROWS)
    return jnp.transpose(total, (1, 0))

def reference(pooled_grad, bag_ids, bag_lengths, table_rows, row_state):
    row_grad = lax.map(table_gradient, (pooled_grad, bag_ids, bag_lengths))
    new_state = row_state + lax.optimization_barrier(jnp.sum(row_grad * row_grad, axis=1)) / WIDTH
    new_rows = table_rows - learning_rate * row_grad / (jnp.sqrt(new_state)[:, None, :] + epsilon)
    return (new_rows, new_state)
```

```python
import jax
import jax.numpy as jnp
from jax import lax
from jax.experimental import pallas as pl
from jax.experimental.pallas import tpu as pltpu
from jax.sharding import PartitionSpec as P

WIDTH = 1024
learning_rate = 0.1
epsilon = 1e-06

LOW = 128
DIGITS = 8


def words_kernel(ids_ref, lens_ref, words_ref):
    table = pl.program_id(0)
    ids = ids_ref[0]
    lens = lens_ref[pl.ds(table, 1), :]
    samples = ids.shape[1]
    word = lax.broadcasted_iota(jnp.int32, (LOW, samples), 0)
    place = lax.broadcasted_iota(jnp.int32, ids.shape, 0)
    unit = jnp.where(place < lens, lax.shift_left(jnp.int32(1), (ids >> 7) * 4), 0)
    low = ids & (LOW - 1)
    total = jnp.zeros((LOW, samples), jnp.int32)
    for position in range(ids.shape[0]):
        total = total + jnp.where(
            low[position : position + 1] == word, unit[position : position + 1], 0
        )
    words_ref[0] = total


def count_words(ids, lens, block=2048):
    tables, places, samples = ids.shape
    return pl.pallas_call(
        words_kernel,
        grid=(tables, samples // block),
        in_specs=[
            pl.BlockSpec((1, places, block), lambda t, i: (t, 0, i)),
            pl.BlockSpec((tables, block), lambda t, i: (0, i)),
        ],
        out_specs=pl.BlockSpec((1, LOW, block), lambda t, i: (t, 0, i)),
        out_shape=jax.ShapeDtypeStruct((tables, LOW, samples), jnp.int32),
        cost_estimate=pl.CostEstimate(
            flops=40_000_000, bytes_accessed=8_000_000, transcendentals=0
        ),
        name="count_words",
    )(ids, lens)


def gradient_kernel(arrived_ref, words_ref, grad_ref, square_ref):
    step = pl.program_id(1)

    @pl.when(step == 0)
    def _():
        grad_ref[...] = jnp.zeros_like(grad_ref)

    grads = jnp.concatenate(
        [arrived_ref[j, 0] for j in range(arrived_ref.shape[0])], axis=1
    )
    words = words_ref[0]
    for digit in range(DIGITS):
        counts = lax.shift_right_logical(words, 4 * digit) & 15
        counts = counts.astype(jnp.float32).astype(jnp.bfloat16)
        grad_ref[0, :, LOW * digit : LOW * (digit + 1)] += lax.dot_general(
            grads, counts, (((1,), (1,)), ((), ())), preferred_element_type=jnp.float32
        )

    @pl.when(step == pl.num_programs(1) - 1)
    def _():
        grad = grad_ref[0]
        square_ref[0] = jnp.sum(grad * grad, axis=0, keepdims=True)


def gradients(arrived, words, block=16):
    sources, tables, columns, owned = arrived.shape
    rows = LOW * DIGITS
    return pl.pallas_call(
        gradient_kernel,
        grid=(tables, sources // block),
        in_specs=[
            pl.BlockSpec((block, 1, columns, owned), lambda t, i: (i, t, 0, 0)),
            pl.BlockSpec((1, LOW, owned * block), lambda t, i: (t, 0, i)),
        ],
        out_specs=[
            pl.BlockSpec((1, columns, rows), lambda t, i: (t, 0, 0)),
            pl.BlockSpec((1, 1, rows), lambda t, i: (t, 0, 0)),
        ],
        out_shape=[
            jax.ShapeDtypeStruct((tables, columns, rows), jnp.float32),
            jax.ShapeDtypeStruct((tables, 1, rows), jnp.float32),
        ],
        cost_estimate=pl.CostEstimate(
            flops=2_147_483_648, bytes_accessed=12_000_000, transcendentals=0
        ),
        name="gradients",
    )(arrived, words)


def body(pooled_grad, bag_ids, bag_lengths, table_rows, row_state):
    members, _, row_count = table_rows.shape
    columns, owned = pooled_grad.shape[1:]
    groups = lax.axis_size("tables")
    splits = lax.axis_size("cols")
    grouped = pooled_grad.reshape(groups, members, columns, owned)
    arrived = lax.all_to_all(grouped, "tables", 0, 0, tiled=True)
    words = count_words(bag_ids, bag_lengths)
    gradient, squares = gradients(arrived, words)
    squares = squares.reshape(members, row_count)
    shared = jnp.broadcast_to(squares[None], (splits, members, row_count))
    totals = jnp.sum(lax.all_to_all(shared, "cols", 0, 0, tiled=True), axis=0)
    new_state = row_state + totals / WIDTH
    new_rows = table_rows - learning_rate * gradient / (
        jnp.sqrt(new_state)[:, None, :] + epsilon
    )
    return (new_rows, new_state)


def solution(mesh):
    placed = (
        P(None, "cols", "tables"),
        P("tables", None, None),
        P("tables", None),
        P("tables", "cols", None),
        P("tables", None),
    )
    return jax.shard_map(
        body,
        mesh=mesh,
        in_specs=placed,
        out_specs=(P("tables", "cols", None), P("tables", None)),
        check_vma=False,
    )
```

```python
import functools

import jax
import jax.numpy as jnp
from jax import lax
from jax.experimental import pallas as pl
from jax.experimental.pallas import tpu as pltpu
from jax.sharding import PartitionSpec as P

WIDTH = 1024
learning_rate = 0.1
epsilon = 1e-06

LOW = 128
DIGITS = 8
STRIDE = 15


def chip_at(place, core, chips):
    return (STRIDE * (place + core * (chips - 1 - 2 * place))) % chips


def place_of(chip, core, chips):
    place = (pow(STRIDE, -1, chips) * chip) % chips
    return place + core * (chips - 1 - 2 * place)


def pack_kernel(core_ref, grads_ref, packed_ref, held, in_done, out_done):
    chips = grads_ref.shape[0]
    reads = in_done.shape[0]
    size = chips // reads
    core = core_ref[0]

    def read(i):
        part = pl.ds(i * size, size)
        return pltpu.make_async_copy(grads_ref.at[part], held.at[part], in_done.at[i])

    def write(chip):
        place = place_of(chip, core, chips)
        return pltpu.make_async_copy(
            held.at[chip], packed_ref.at[place], out_done.at[chip]
        )

    for i in range(reads):
        read(i).start()
    for i in range(reads):
        read(i).wait()
        for chip in range(i * size, (i + 1) * size):
            write(chip).start()
    for chip in range(chips):
        write(chip).wait()


def pack(core, grads):
    return pl.pallas_call(
        pack_kernel,
        in_specs=[
            pl.BlockSpec(memory_space=pltpu.SMEM),
            pl.BlockSpec(memory_space=pl.ANY),
        ],
        out_specs=pl.BlockSpec(memory_space=pl.ANY),
        out_shape=jax.ShapeDtypeStruct(grads.shape, grads.dtype),
        scratch_shapes=[
            pltpu.VMEM(grads.shape, grads.dtype),
            pltpu.SemaphoreType.DMA((4,)),
            pltpu.SemaphoreType.DMA((grads.shape[0],)),
        ],
        cost_estimate=pl.CostEstimate(
            flops=0, bytes_accessed=4 * grads.size, transcendentals=0
        ),
        name="pack",
    )(core, grads)


def words_kernel(chips, owned, table, half, core_ref, ids_ref, lens_ref, words_ref):
    block = pl.program_id(0)
    source_core = core_ref[0] if half == 0 else 1 - core_ref[0]
    places = words_ref.shape[0] // owned
    word = lax.broadcasted_iota(jnp.int32, (LOW, owned), 0)
    for i in range(places):
        chip = chip_at(block * places + i, source_core, chips)
        start = pl.multiple_of((2 * chip + source_core) * owned, owned)
        ids = ids_ref[0, :, pl.ds(start, owned)]
        lens = lens_ref[:, pl.ds(start, owned)][table : table + 1]
        position = lax.broadcasted_iota(jnp.int32, ids.shape, 0)
        unit = jnp.where(
            position < lens, lax.shift_left(jnp.int32(1), (ids >> 7) * 4), 0
        )
        low = ids & (LOW - 1)
        total = jnp.zeros((LOW, owned), jnp.int32)
        for k in range(ids.shape[0]):
            total = total + jnp.where(low[k : k + 1] == word, unit[k : k + 1], 0)
        words_ref[owned * i : owned * (i + 1), :] = total.T


def count_words(core, ids, lens, chips, owned, table, half, block=8):
    tables, positions, samples = ids.shape
    return pl.pallas_call(
        functools.partial(words_kernel, chips, owned, table, half),
        grid=(chips // block,),
        in_specs=[
            pl.BlockSpec(memory_space=pltpu.SMEM),
            pl.BlockSpec((1, positions, samples), lambda i: (table, 0, 0)),
            pl.BlockSpec((tables, samples), lambda i: (0, 0)),
        ],
        out_specs=pl.BlockSpec((block * owned, LOW), lambda i: (i, 0)),
        out_shape=jax.ShapeDtypeStruct((chips * owned, LOW), jnp.int32),
        cost_estimate=pl.CostEstimate(
            flops=15_000_000, bytes_accessed=2_500_000, transcendentals=0
        ),
        name=f"count_words_{table}_{half}",
    )(core, ids, lens)


def multiply(arrived, words):
    grads = jnp.concatenate([arrived[j] for j in range(arrived.shape[0])], axis=1)
    products = []
    for pair in range(DIGITS // 2):
        counts, scales = [], []
        for digit in (2 * pair, 2 * pair + 1):
            top = digit == DIGITS - 1
            if top:
                held = lax.shift_right_logical(words, 4 * digit)
            else:
                held = words & (15 << (4 * digit))
            counts.append(held.astype(jnp.float32).astype(jnp.bfloat16))
            scales.append(1.0 if top else 16.0**-digit)
        product = jnp.dot(
            grads, jnp.concatenate(counts, axis=1), preferred_element_type=jnp.float32
        )
        lane = lax.broadcasted_iota(jnp.int32, product.shape, 1)
        products.append(product * jnp.where(lane < LOW, scales[0], scales[1]))
    return products


def part(pair):
    return slice(2 * LOW * pair, 2 * LOW * (pair + 1))


def own_kernel(table, core_ref, arrived_ref, words_ref, grad_ref):
    core = core_ref[0]
    arrived = [arrived_ref[j, core, table] for j in range(arrived_ref.shape[0])]
    for pair, product in enumerate(multiply(jnp.stack(arrived), words_ref[...])):
        grad_ref[:, part(pair)] = product


def own_half(core, arrived, words, table):
    columns = arrived.shape[3]
    return pl.pallas_call(
        functools.partial(own_kernel, table),
        in_specs=[
            pl.BlockSpec(memory_space=pltpu.SMEM),
            pl.BlockSpec(memory_space=pltpu.VMEM),
            pl.BlockSpec(memory_space=pltpu.VMEM),
        ],
        out_specs=pl.BlockSpec(memory_space=pltpu.VMEM),
        out_shape=jax.ShapeDtypeStruct((columns, LOW * DIGITS), jnp.float32),
        cost_estimate=pl.CostEstimate(
            flops=536_870_912, bytes_accessed=3_000_000, transcendentals=0
        ),
        compiler_params=pltpu.CompilerParams(vmem_limit_bytes=24 << 20),
        name=f"own_half_{table}",
    )(core, arrived, words)


def sibling_kernel(tables, *refs):
    arrived_ref = refs[0]
    words_refs, first_refs = refs[1 : 1 + tables], refs[1 + tables : 1 + 2 * tables]
    grad_ref, square_ref = refs[1 + 2 * tables :]
    for table in range(tables):
        products = multiply(arrived_ref[:, table], words_refs[table][...])
        for pair, product in enumerate(products):
            product = product + first_refs[table][:, part(pair)]
            grad_ref[table, :, part(pair)] = product
            square = jnp.sum(product * product, axis=0, keepdims=True)
            for copy in range(square_ref.shape[0]):
                square_ref[copy, table : table + 1, part(pair)] = square


def sibling_half(arrived, words, first, copies):
    _, tables, columns, _ = arrived.shape
    rows = LOW * DIGITS
    return pl.pallas_call(
        functools.partial(sibling_kernel, tables),
        in_specs=[pl.BlockSpec(memory_space=pltpu.VMEM)] * (1 + 2 * tables),
        out_specs=[pl.BlockSpec(memory_space=pltpu.VMEM)] * 2,
        out_shape=[
            jax.ShapeDtypeStruct((tables, columns, rows), jnp.float32),
            jax.ShapeDtypeStruct((copies, tables, rows), jnp.float32),
        ],
        cost_estimate=pl.CostEstimate(
            flops=1_073_741_824, bytes_accessed=6_000_000, transcendentals=0
        ),
        compiler_params=pltpu.CompilerParams(vmem_limit_bytes=24 << 20),
        name="sibling_half",
    )(arrived, *words, *first)


def body(pooled_grad, bag_ids, bag_lengths, table_rows, row_state):
    members = table_rows.shape[0]
    columns, owned = pooled_grad.shape[1:]
    groups = lax.axis_size("tables")
    splits = lax.axis_size("cols")
    chips = groups // 2
    core = (lax.axis_index("tables") % 2).astype(jnp.int32).reshape(1)
    orders = [
        [2 * chip_at(place, c, chips) + c for place in range(chips)] for c in range(2)
    ]
    grouped = pooled_grad.reshape(chips, 2, members, columns, owned)
    arrived = lax.all_to_all(
        pack(core, grouped), "tables", 0, 0, tiled=True, axis_index_groups=orders
    )
    words = [
        [
            count_words(core, bag_ids, bag_lengths, chips, owned, table, half)
            for table in range(members)
        ]
        for half in range(2)
    ]
    arrived, words = lax.optimization_barrier((arrived, words))
    other = lax.dynamic_index_in_dim(arrived, 1 - core[0], 1, keepdims=False)
    swapped = lax.ppermute(other, "tables", [(k, k ^ 1) for k in range(groups)])
    first = [own_half(core, arrived, words[0][table], table) for table in range(members)]
    gradient, squares = sibling_half(swapped, words[1], first, splits)
    totals = jnp.sum(lax.all_to_all(squares, "cols", 0, 0, tiled=True), axis=0)
    new_state = row_state + totals / WIDTH
    scale = learning_rate / (jnp.sqrt(new_state) + epsilon)
    new_rows = table_rows - scale[:, None, :] * gradient
    return (new_rows, new_state)


def solution(mesh):
    placed = (
        P(None, "cols", "tables"),
        P("tables", None, None),
        P("tables", None),
        P("tables", "cols", None),
        P("tables", None),
    )
    return jax.shard_map(
        body,
        mesh=mesh,
        in_specs=placed,
        out_specs=(P("tables", "cols", None), P("tables", None)),
        check_vma=False,
    )
```

```python
import functools

import jax
import jax.numpy as jnp
from jax import lax
from jax.experimental import pallas as pl
from jax.experimental.pallas import tpu as pltpu
from jax.sharding import PartitionSpec as P

WIDTH = 1024
learning_rate = 0.1
epsilon = 1e-06

LOW = 128
DIGITS = 8


def chip_at(place, core, chips):
    return (place + core * (chips // 2)) % chips


def pack_kernel(core_ref, grads_ref, packed_ref, held, in_done, out_done):
    chips = grads_ref.shape[0]
    parts = in_done.shape[0]
    size = chips // parts
    core = core_ref[0]

    def read(i):
        return pltpu.make_async_copy(
            grads_ref.at[pl.ds(chip_at(i * size, core, chips), size)],
            held.at[pl.ds(i * size, size)],
            in_done.at[i],
        )

    def write(i):
        part = pl.ds(i * size, size)
        return pltpu.make_async_copy(held.at[part], packed_ref.at[part], out_done.at[i])

    for i in range(parts):
        read(i).start()
    for i in range(parts):
        read(i).wait()
        write(i).start()
    for i in range(parts):
        write(i).wait()


def pack(core, grads, parts=8):
    return pl.pallas_call(
        pack_kernel,
        in_specs=[
            pl.BlockSpec(memory_space=pltpu.SMEM),
            pl.BlockSpec(memory_space=pl.ANY),
        ],
        out_specs=pl.BlockSpec(memory_space=pl.ANY),
        out_shape=jax.ShapeDtypeStruct(grads.shape, grads.dtype),
        scratch_shapes=[
            pltpu.VMEM(grads.shape, grads.dtype),
            pltpu.SemaphoreType.DMA((parts,)),
            pltpu.SemaphoreType.DMA((parts,)),
        ],
        cost_estimate=pl.CostEstimate(
            flops=0, bytes_accessed=4 * grads.size, transcendentals=0
        ),
        name="pack",
    )(core, grads)


def words_kernel(chips, owned, table, half, core_ref, ids_ref, lens_ref, words_ref):
    block = pl.program_id(0)
    source_core = core_ref[0] if half == 0 else 1 - core_ref[0]
    places = words_ref.shape[0] // owned
    word = lax.broadcasted_iota(jnp.int32, (LOW, owned), 0)
    for i in range(places):
        chip = chip_at(block * places + i, source_core, chips)
        start = pl.multiple_of((2 * chip + source_core) * owned, owned)
        ids = ids_ref[0, :, pl.ds(start, owned)]
        lens = lens_ref[:, pl.ds(start, owned)][table : table + 1]
        position = lax.broadcasted_iota(jnp.int32, ids.shape, 0)
        unit = jnp.where(
            position < lens, lax.shift_left(jnp.int32(1), (ids >> 7) * 4), 0
        )
        low = ids & (LOW - 1)
        total = jnp.zeros((LOW, owned), jnp.int32)
        for k in range(ids.shape[0]):
            total = total + jnp.where(low[k : k + 1] == word, unit[k : k + 1], 0)
        words_ref[owned * i : owned * (i + 1), :] = total.T


def count_words(core, ids, lens, chips, owned, table, half, block=8):
    tables, positions, samples = ids.shape
    return pl.pallas_call(
        functools.partial(words_kernel, chips, owned, table, half),
        grid=(chips // block,),
        in_specs=[
            pl.BlockSpec(memory_space=pltpu.SMEM),
            pl.BlockSpec((1, positions, samples), lambda i: (table, 0, 0)),
            pl.BlockSpec((tables, samples), lambda i: (0, 0)),
        ],
        out_specs=pl.BlockSpec((block * owned, LOW), lambda i: (i, 0)),
        out_shape=jax.ShapeDtypeStruct((chips * owned, LOW), jnp.int32),
        cost_estimate=pl.CostEstimate(
            flops=15_000_000, bytes_accessed=2_500_000, transcendentals=0
        ),
        name=f"count_words_{table}_{half}",
    )(core, ids, lens)


def multiply(arrived, words):
    grads = jnp.concatenate([arrived[j] for j in range(arrived.shape[0])], axis=1)
    products = []
    for pair in range(DIGITS // 2):
        counts, scales = [], []
        for digit in (2 * pair, 2 * pair + 1):
            top = digit == DIGITS - 1
            if top:
                held = lax.shift_right_logical(words, 4 * digit)
            else:
                held = words & (15 << (4 * digit))
            counts.append(held.astype(jnp.float32).astype(jnp.bfloat16))
            scales.append(1.0 if top else 16.0**-digit)
        product = jnp.dot(
            grads, jnp.concatenate(counts, axis=1), preferred_element_type=jnp.float32
        )
        lane = lax.broadcasted_iota(jnp.int32, product.shape, 1)
        products.append(product * jnp.where(lane < LOW, scales[0], scales[1]))
    return products


def part(pair):
    return slice(2 * LOW * pair, 2 * LOW * (pair + 1))


def own_kernel(table, core_ref, arrived_ref, words_ref, grad_ref):
    core = core_ref[0]
    arrived = [arrived_ref[j, core, table] for j in range(arrived_ref.shape[0])]
    for pair, product in enumerate(multiply(jnp.stack(arrived), words_ref[...])):
        grad_ref[:, part(pair)] = product


def own_half(core, arrived, words, table):
    columns = arrived.shape[3]
    return pl.pallas_call(
        functools.partial(own_kernel, table),
        in_specs=[
            pl.BlockSpec(memory_space=pltpu.SMEM),
            pl.BlockSpec(memory_space=pltpu.VMEM),
            pl.BlockSpec(memory_space=pltpu.VMEM),
        ],
        out_specs=pl.BlockSpec(memory_space=pltpu.VMEM),
        out_shape=jax.ShapeDtypeStruct((columns, LOW * DIGITS), jnp.float32),
        cost_estimate=pl.CostEstimate(
            flops=536_870_912, bytes_accessed=3_000_000, transcendentals=0
        ),
        compiler_params=pltpu.CompilerParams(vmem_limit_bytes=24 << 20),
        name=f"own_half_{table}",
    )(core, arrived, words)


def sibling_kernel(tables, *refs):
    arrived_ref = refs[0]
    words_refs, first_refs = refs[1 : 1 + tables], refs[1 + tables : 1 + 2 * tables]
    grad_ref, square_ref = refs[1 + 2 * tables :]
    for table in range(tables):
        products = multiply(arrived_ref[:, table], words_refs[table][...])
        for pair, product in enumerate(products):
            product = product + first_refs[table][:, part(pair)]
            grad_ref[table, :, part(pair)] = product
            square = jnp.sum(product * product, axis=0, keepdims=True)
            for copy in range(square_ref.shape[0]):
                square_ref[copy, table : table + 1, part(pair)] = square


def sibling_half(arrived, words, first, copies):
    _, tables, columns, _ = arrived.shape
    rows = LOW * DIGITS
    return pl.pallas_call(
        functools.partial(sibling_kernel, tables),
        in_specs=[pl.BlockSpec(memory_space=pltpu.VMEM)] * (1 + 2 * tables),
        out_specs=[pl.BlockSpec(memory_space=pltpu.VMEM)] * 2,
        out_shape=[
            jax.ShapeDtypeStruct((tables, columns, rows), jnp.float32),
            jax.ShapeDtypeStruct((copies, tables, rows), jnp.float32),
        ],
        cost_estimate=pl.CostEstimate(
            flops=1_073_741_824, bytes_accessed=6_000_000, transcendentals=0
        ),
        compiler_params=pltpu.CompilerParams(vmem_limit_bytes=24 << 20),
        name="sibling_half",
    )(arrived, *words, *first)


def update_kernel(shared_ref, state_ref, grad_ref, rows_ref, new_rows_ref, new_state_ref):
    total = shared_ref[0]
    for copy in range(1, shared_ref.shape[0]):
        total = total + shared_ref[copy]
    new_state = state_ref[...] + total / WIDTH
    new_state_ref[...] = new_state
    scale = learning_rate / (jnp.sqrt(new_state) + epsilon)
    for table in range(rows_ref.shape[0]):
        new_rows_ref[table] = rows_ref[table] - scale[table : table + 1] * grad_ref[table]


def update(shared, state, gradient, rows):
    return pl.pallas_call(
        update_kernel,
        in_specs=[pl.BlockSpec(memory_space=pltpu.VMEM)] * 4,
        out_specs=[pl.BlockSpec(memory_space=pltpu.VMEM)] * 2,
        out_shape=[
            jax.ShapeDtypeStruct(rows.shape, jnp.float32),
            jax.ShapeDtypeStruct(state.shape, jnp.float32),
        ],
        cost_estimate=pl.CostEstimate(
            flops=3 * rows.size, bytes_accessed=12 * rows.size, transcendentals=0
        ),
        compiler_params=pltpu.CompilerParams(vmem_limit_bytes=24 << 20),
        name="update",
    )(shared, state, gradient, rows)


def body(pooled_grad, bag_ids, bag_lengths, table_rows, row_state):
    members = table_rows.shape[0]
    columns, owned = pooled_grad.shape[1:]
    groups = lax.axis_size("tables")
    splits = lax.axis_size("cols")
    chips = groups // 2
    core = (lax.axis_index("tables") % 2).astype(jnp.int32).reshape(1)
    orders = [
        [2 * chip_at(place, c, chips) + c for place in range(chips)] for c in range(2)
    ]
    grouped = pooled_grad.reshape(chips, 2, members, columns, owned)
    arrived = lax.all_to_all(
        pack(core, grouped), "tables", 0, 0, tiled=True, axis_index_groups=orders
    )
    words = [
        [
            count_words(core, bag_ids, bag_lengths, chips, owned, table, half)
            for table in range(members)
        ]
        for half in range(2)
    ]
    arrived, words = lax.optimization_barrier((arrived, words))
    other = lax.dynamic_index_in_dim(arrived, 1 - core[0], 1, keepdims=False)
    swapped = lax.ppermute(other, "tables", [(k, k ^ 1) for k in range(groups)])
    first = [own_half(core, arrived, words[0][table], table) for table in range(members)]
    gradient, squares = sibling_half(swapped, words[1], first, splits)
    shared = lax.all_to_all(squares, "cols", 0, 0, tiled=True)
    new_rows, new_state = update(shared, row_state, gradient, table_rows)
    return (new_rows, new_state)


def solution(mesh):
    placed = (
        P(None, "cols", "tables"),
        P("tables", None, None),
        P("tables", None),
        P("tables", "cols", None),
        P("tables", None),
    )
    return jax.shard_map(
        body,
        mesh=mesh,
        in_specs=placed,
        out_specs=(P("tables", "cols", None), P("tables", None)),
        check_vma=False,
    )
```

```python
import functools

import jax
import jax.numpy as jnp
from jax import lax
from jax.experimental import pallas as pl
from jax.experimental.pallas import tpu as pltpu
from jax.sharding import PartitionSpec as P

WIDTH = 1024
learning_rate = 0.1
epsilon = 1e-06

LOW = 128
DIGITS = 8


def chip_at(place, core, chips):
    return (place + core * (chips // 2)) % chips


def pack_kernel(core_ref, grads_ref, packed_ref, held, in_done, out_done):
    chips = grads_ref.shape[0]
    parts = in_done.shape[0]
    size = chips // parts
    core = core_ref[0]

    def read(i):
        return pltpu.make_async_copy(
            grads_ref.at[pl.ds(chip_at(i * size, core, chips), size)],
            held.at[pl.ds(i * size, size)],
            in_done.at[i],
        )

    def write(i):
        part = pl.ds(i * size, size)
        return pltpu.make_async_copy(held.at[part], packed_ref.at[part], out_done.at[i])

    for i in range(parts):
        read(i).start()
    for i in range(parts):
        read(i).wait()
        write(i).start()
    for i in range(parts):
        write(i).wait()


def pack(core, grads, parts=8):
    return pl.pallas_call(
        pack_kernel,
        in_specs=[
            pl.BlockSpec(memory_space=pltpu.SMEM),
            pl.BlockSpec(memory_space=pl.ANY),
        ],
        out_specs=pl.BlockSpec(memory_space=pl.ANY),
        out_shape=jax.ShapeDtypeStruct(grads.shape, grads.dtype),
        scratch_shapes=[
            pltpu.VMEM(grads.shape, grads.dtype),
            pltpu.SemaphoreType.DMA((parts,)),
            pltpu.SemaphoreType.DMA((parts,)),
        ],
        cost_estimate=pl.CostEstimate(
            flops=0, bytes_accessed=4 * grads.size, transcendentals=0
        ),
        name="pack",
    )(core, grads)


def counts_kernel(chips, owned, table, half, core_ref, ids_ref, lens_ref, counts_ref):
    block = pl.program_id(0)
    source_core = core_ref[0] if half == 0 else 1 - core_ref[0]
    places = counts_ref.shape[0] // owned
    word = lax.broadcasted_iota(jnp.int32, (LOW, owned), 0)
    for i in range(places):
        chip = chip_at(block * places + i, source_core, chips)
        start = pl.multiple_of((2 * chip + source_core) * owned, owned)
        ids = ids_ref[0, :, pl.ds(start, owned)]
        lens = lens_ref[:, pl.ds(start, owned)][table : table + 1]
        position = lax.broadcasted_iota(jnp.int32, ids.shape, 0)
        unit = jnp.where(
            position < lens, lax.shift_left(jnp.int32(1), (ids >> 7) * 4), 0
        )
        low = ids & (LOW - 1)
        total = jnp.zeros((LOW, owned), jnp.int32)
        for k in range(ids.shape[0]):
            total = total + jnp.where(low[k : k + 1] == word, unit[k : k + 1], 0)
        words = total.T
        samples = pl.ds(owned * i, owned)
        if counts_ref.dtype == jnp.int32:
            counts_ref[samples, :] = words
        else:
            for digit in range(DIGITS):
                count = lax.shift_right_logical(words, 4 * digit) & 15
                counts_ref[samples, pl.ds(LOW * digit, LOW)] = count.astype(
                    jnp.float32
                ).astype(counts_ref.dtype)


def count(core, ids, lens, chips, owned, table, half, packed, block=8):
    tables, positions, samples = ids.shape
    width, dtype = (LOW, jnp.int32) if packed else (LOW * DIGITS, jnp.float8_e5m2)
    return pl.pallas_call(
        functools.partial(counts_kernel, chips, owned, table, half),
        grid=(chips // block,),
        in_specs=[
            pl.BlockSpec(memory_space=pltpu.SMEM),
            pl.BlockSpec((1, positions, samples), lambda i: (table, 0, 0)),
            pl.BlockSpec((tables, samples), lambda i: (0, 0)),
        ],
        out_specs=pl.BlockSpec((block * owned, width), lambda i: (i, 0)),
        out_shape=jax.ShapeDtypeStruct((chips * owned, width), dtype),
        cost_estimate=pl.CostEstimate(
            flops=15_000_000, bytes_accessed=4_000_000, transcendentals=0
        ),
        name=f"count_{table}_{half}",
    )(core, ids, lens)


def part(pair):
    return slice(2 * LOW * pair, 2 * LOW * (pair + 1))


def multiply(arrived, counts_ref):
    grads = jnp.concatenate([arrived[j] for j in range(arrived.shape[0])], axis=1)
    products = []
    for pair in range(DIGITS // 2):
        if counts_ref.dtype != jnp.int32:
            products.append(
                jnp.dot(
                    grads, counts_ref[:, part(pair)], preferred_element_type=jnp.float32
                )
            )
            continue
        words = counts_ref[...]
        counts, scales = [], []
        for digit in (2 * pair, 2 * pair + 1):
            top = digit == DIGITS - 1
            if top:
                held = lax.shift_right_logical(words, 4 * digit)
            else:
                held = words & (15 << (4 * digit))
            counts.append(held.astype(jnp.float32).astype(jnp.bfloat16))
            scales.append(1.0 if top else 16.0**-digit)
        product = jnp.dot(
            grads, jnp.concatenate(counts, axis=1), preferred_element_type=jnp.float32
        )
        lane = lax.broadcasted_iota(jnp.int32, product.shape, 1)
        products.append(product * jnp.where(lane < LOW, scales[0], scales[1]))
    return products


def own_kernel(table, core_ref, arrived_ref, counts_ref, grad_ref):
    core = core_ref[0]
    arrived = [arrived_ref[j, core, table] for j in range(arrived_ref.shape[0])]
    for pair, product in enumerate(multiply(jnp.stack(arrived), counts_ref)):
        grad_ref[:, part(pair)] = product


def own_half(core, arrived, counts, table):
    columns = arrived.shape[3]
    vmem = pl.BlockSpec(memory_space=pltpu.VMEM)
    return pl.pallas_call(
        functools.partial(own_kernel, table),
        in_specs=[pl.BlockSpec(memory_space=pltpu.SMEM), vmem, vmem],
        out_specs=vmem,
        out_shape=jax.ShapeDtypeStruct((columns, LOW * DIGITS), jnp.float32),
        cost_estimate=pl.CostEstimate(
            flops=536_870_912, bytes_accessed=3_000_000, transcendentals=0
        ),
        compiler_params=pltpu.CompilerParams(vmem_limit_bytes=24 << 20),
        name=f"own_half_{table}",
    )(core, arrived, counts)


def sibling_kernel(table, arrived_ref, counts_ref, first_ref, *refs):
    earlier, (grad_ref, square_ref) = refs[:-2], refs[-2:]
    last = len(square_ref.shape) == 3
    for pair, product in enumerate(multiply(arrived_ref[:, table], counts_ref)):
        product = product + first_ref[:, part(pair)]
        grad_ref[:, part(pair)] = product
        square = jnp.sum(product * product, axis=0, keepdims=True)
        if not last:
            square_ref[:, part(pair)] = square
            continue
        squares = [ref[:, part(pair)] for ref in earlier] + [square]
        for copy in range(square_ref.shape[0]):
            for row, value in enumerate(squares):
                square_ref[copy, row : row + 1, part(pair)] = value


def sibling_half(arrived, counts, first, copies):
    tables, columns = arrived.shape[1:3]
    rows = LOW * DIGITS
    vmem = pl.BlockSpec(memory_space=pltpu.VMEM)
    gradients, squares = [], []
    for table in range(tables):
        earlier = squares if table == tables - 1 else []
        shape = (copies, tables, rows) if table == tables - 1 else (1, rows)
        gradient, square = pl.pallas_call(
            functools.partial(sibling_kernel, table),
            in_specs=[vmem] * (3 + len(earlier)),
            out_specs=[vmem] * 2,
            out_shape=[
                jax.ShapeDtypeStruct((columns, rows), jnp.float32),
                jax.ShapeDtypeStruct(shape, jnp.float32),
            ],
            cost_estimate=pl.CostEstimate(
                flops=536_870_912, bytes_accessed=5_000_000, transcendentals=0
            ),
            compiler_params=pltpu.CompilerParams(vmem_limit_bytes=24 << 20),
            name=f"sibling_half_{table}",
        )(arrived, counts[table], first[table], *earlier)
        gradients.append(gradient)
        squares = squares + [square]
    return gradients, squares[-1]


def update_kernel(shared_ref, state_ref, rows_ref, *refs):
    grad_refs, (new_rows_ref, new_state_ref) = refs[:-2], refs[-2:]
    total = shared_ref[0]
    for copy in range(1, shared_ref.shape[0]):
        total = total + shared_ref[copy]
    new_state = state_ref[...] + total / WIDTH
    new_state_ref[...] = new_state
    scale = learning_rate / (jnp.sqrt(new_state) + epsilon)
    for table in range(rows_ref.shape[0]):
        step = scale[table : table + 1] * grad_refs[table][...]
        new_rows_ref[table] = rows_ref[table] - step


def update(shared, state, rows, gradients):
    return pl.pallas_call(
        update_kernel,
        in_specs=[pl.BlockSpec(memory_space=pltpu.VMEM)] * (3 + len(gradients)),
        out_specs=[pl.BlockSpec(memory_space=pltpu.VMEM)] * 2,
        out_shape=[
            jax.ShapeDtypeStruct(rows.shape, jnp.float32),
            jax.ShapeDtypeStruct(state.shape, jnp.float32),
        ],
        cost_estimate=pl.CostEstimate(
            flops=3 * rows.size, bytes_accessed=12 * rows.size, transcendentals=0
        ),
        compiler_params=pltpu.CompilerParams(vmem_limit_bytes=24 << 20),
        name="update",
    )(shared, state, rows, *gradients)


def body(pooled_grad, bag_ids, bag_lengths, table_rows, row_state):
    members = table_rows.shape[0]
    columns, owned = pooled_grad.shape[1:]
    groups = lax.axis_size("tables")
    splits = lax.axis_size("cols")
    chips = groups // 2
    core = (lax.axis_index("tables") % 2).astype(jnp.int32).reshape(1)
    orders = [
        [2 * chip_at(place, c, chips) + c for place in range(chips)] for c in range(2)
    ]
    grouped = pooled_grad.reshape(chips, 2, members, columns, owned)
    arrived = lax.all_to_all(
        pack(core, grouped), "tables", 0, 0, tiled=True, axis_index_groups=orders
    )
    counts = [
        [
            count(
                core,
                bag_ids,
                bag_lengths,
                chips,
                owned,
                table,
                half,
                packed=half == 0 or table < members - 1,
            )
            for table in range(members)
        ]
        for half in range(2)
    ]
    arrived, counts = lax.optimization_barrier((arrived, counts))
    other = lax.dynamic_index_in_dim(arrived, 1 - core[0], 1, keepdims=False)
    swapped = lax.ppermute(other, "tables", [(k, k ^ 1) for k in range(groups)])
    first = [
        own_half(core, arrived, counts[0][table], table) for table in range(members)
    ]
    gradients, squares = sibling_half(swapped, counts[1], first, splits)
    shared = lax.all_to_all(squares, "cols", 0, 0, tiled=True)
    new_rows, new_state = update(shared, row_state, table_rows, gradients)
    return (new_rows, new_state)


def solution(mesh):
    placed = (
        P(None, "cols", "tables"),
        P("tables", None, None),
        P("tables", None),
        P("tables", "cols", None),
        P("tables", None),
    )
    return jax.shard_map(
        body,
        mesh=mesh,
        in_specs=placed,
        out_specs=(P("tables", "cols", None), P("tables", None)),
        check_vma=False,
    )
```
